32 devices in a mesh: group: 2 (over y), node: 4 (over z), local: 2 (over x), pair: 2 (over core).
Axes of the slice: x: 2, y: 2, z: 4, core: 2. Of those that a mesh axis runs over, the one named last changes fastest.
Arguments:
- tokens: bfloat16 [512, 3584], P(('group', 'node', 'local', 'pair')), parts along dimension 0, may hold values from -6 to 6
- expert_ids: int32 [512, 8], P(('group', 'node', 'local', 'pair')), parts along dimension 0, may hold values from 0 to 15, all different within a row; in each aligned block of 16 rows (0 to 15, 16 to 31, ...) at most 16 rows name the same one
- combine_weights: bfloat16 [512, 8], P(('group', 'node', 'local', 'pair')), parts along dimension 0, may hold values from 0.099609375 to 1
- expert_weight: bfloat16 [16, 3584, 1024], P(('node', 'local', 'pair')), may hold values from -0.09375 to 0.09375
- query_latent: bfloat16 [512, 64, 512], P(('group', 'node', 'local', 'pair')), parts along dimension 0
- query_rope: bfloat16 [512, 4096], P(('group', 'node', 'local', 'pair')), parts along dimension 0
- cache_latent: bfloat16 [512, 128, 512], P(('group', 'node', 'local', 'pair')), parts along dimension 0
- cache_rope: bfloat16 [512, 64, 128], P(('group', 'node', 'local', 'pair')), parts along dimension 0
- lengths: int32 [512], P(('group', 'node', 'local', 'pair')), parts along dimension 0, may hold values from 2 to 128, as said below
Outputs:
- expert_mix: bfloat16 [512, 1024], P(('group', 'node', 'local', 'pair')), parts along dimension 0
- attended: bfloat16 [512, 64, 512], P(('group', 'node', 'local', 'pair')), parts along dimension 0
The draws below stay inside these ranges and needn't reach their ends.
There are 2 independent parts, one for each index of `group`. The reference program is written for one: setup_inputs(seed, part) draws one part's arguments, and reference() takes and returns one part's arrays. A program takes and returns all parts, laid end to end along the dimension named above; an argument that names none is the same for every part. Nothing has to cross between parts.
Inputs may be any that keep to these rules, and one draw needn't show every extreme that they name: `expert_ids`: each row names 8 different experts; in each aligned block of 16 rows (one device's tokens) no expert is named by more than 16 rows, a bound that some block reaches. `lengths`: some sequence holds exactly 128 positions.
All inputs are finite; a program needn't handle non-finite values.
Results may differ from the reference program's by a relative error of at most 0.0085.
Values may be sent and summed in bfloat16 or wider, within the bound.
No kernel may reach another device: no remote copies, remote signals or barrier semaphores. Data moves between devices by JAX's collectives and lax.ppermute only.
A program may use at most 64 MiB of HBM per device.

```python
import math
import jax
import jax.numpy as jnp
import numpy as np
from jax import lax

D = 3584
H = 1024
HEADS = 64
LATENT = 512
ROPE = 64
TOPK = 8
ROWS = 16
LMAX = 128
EXPERTS = 16
CAP = 16
TOKENS = 256
N_NODE = 4
N_LOCAL = 2
N_PAIR = 2


score_scale = 192.0 ** (-0.5)


def attention_parts(key, strength_on):
    subkeys = jax.random.split(key, 4)
    q_lat = jax.random.normal(subkeys[0], (TOKENS, HEADS, LATENT), jnp.float32)
    q_rot = jax.random.normal(subkeys[1], (TOKENS, HEADS, ROPE), jnp.float32)
    k_lat = jax.random.normal(subkeys[2], (TOKENS, LMAX, LATENT), jnp.float32)
    k_rot = jax.random.normal(subkeys[3], (TOKENS, LMAX, ROPE), jnp.float32)
    row_ids = jnp.arange(TOKENS, dtype=jnp.int32)
    chosen = (row_ids % 4 == 0).astype(jnp.float32) * strength_on
    strength = 5.0 + 3.5 * (row_ids // 4 % 3).astype(jnp.float32)
    upper_half = (jnp.arange(LATENT) >= LATENT // 2).astype(jnp.float32)
    sign_flip = 2.0 * upper_half - 1.0
    leading = (jnp.arange(ROPE) == 0).astype(jnp.float32)
    first_lat = k_lat[:, 0, :]
    first_rot = k_rot[:, 0, :] * (1.0 - leading) + leading
    offset_rope = 2.0 / (strength * score_scale)
    second_lat = first_lat * sign_flip
    second_rot = first_rot - leading[None, :] * offset_rope[:, None]
    chosen_rows = chosen[:, None]
    k_rot_first = chosen_rows * first_rot + (1.0 - chosen_rows) * k_rot[:, 0, :]
    k_lat_second = chosen_rows * second_lat + (1.0 - chosen_rows) * k_lat[:, 1, :]
    k_rot_second = chosen_rows * second_rot + (1.0 - chosen_rows) * k_rot[:, 1, :]
    k_lat = k_lat.at[:, 1, :].set(k_lat_second)
    k_rot = k_rot.at[:, 0, :].set(k_rot_first).at[:, 1, :].set(k_rot_second)
    aim_lat = strength[:, None, None] * (first_lat * upper_half[None, :])[:, None, :] * jnp.ones((1, HEADS, 1), jnp.float32)
    aim_rot = strength[:, None, None] * first_rot[:, None, :] * jnp.ones((1, HEADS, 1), jnp.float32)
    chosen_cube = chosen[:, None, None]
    q_lat = chosen_cube * aim_lat + (1.0 - chosen_cube) * q_lat
    q_rot = chosen_cube * aim_rot + (1.0 - chosen_cube) * q_rot
    return (q_lat, q_rot.reshape(TOKENS, HEADS * ROPE), k_lat, jnp.swapaxes(k_rot, 1, 2))


def draw_query_latent(key, part):
    strength_on = 0.0
    return attention_parts(key, strength_on)[0].astype(jnp.bfloat16)


def draw_query_rope(key, part):
    strength_on = 0.0
    return attention_parts(key, strength_on)[1].astype(jnp.bfloat16)


def draw_cache_latent(key, part):
    strength_on = 0.0
    return attention_parts(key, strength_on)[2].astype(jnp.bfloat16)


def draw_cache_rope(key, part):
    strength_on = 0.0
    return attention_parts(key, strength_on)[3].astype(jnp.bfloat16)


def draw_lengths(key, part):
    key = jax.random.fold_in(key, 7)
    values = jax.random.randint(key, (TOKENS,), 2, LMAX + 1, dtype=jnp.int32)
    return values.at[0].set(LMAX)


def level_of(stream_key, dims, cuts, least, top_value):
    def one(dim, blocks):
        heights = jax.random.uniform(jax.random.fold_in(jax.random.fold_in(stream_key, 6), dim), (blocks,), jnp.float32, least / len(cuts), top_value / len(cuts))
        return jnp.repeat(jnp.exp(heights), dims[dim] // blocks).reshape((-1,) + (1,) * (len(dims) - dim - 1))

    level = one(*cuts[0])
    for cut in cuts[1:]:
        level = level * one(*cut)
    return level


def shared_out(key, own, number, rows, count, top, most, skew):
    order = jax.random.permutation(key, count)
    packed, common = load_shares(count, rows * top, most, skew, True), load_shares(count, rows * top, most, skew, False)
    places = jnp.arange(count)

    def named(sizes, offset_by):
        used = int((sizes > 0).sum())
        fixed = max(1, used // 4)
        moved = fixed + (places - fixed + offset_by * (used - fixed)) % max(1, count - fixed)
        return jnp.zeros((count,), jnp.int32).at[order[jnp.where(places < fixed, places, moved)]].set(jnp.asarray(sizes, jnp.int32))

    sizes = jnp.where(number % 4 == 0, named(packed, number // 4), named(common, number - number // 4 - 1))
    mixed = jax.random.permutation(jax.random.fold_in(own, 3), count)
    source_of, taker = mixed[0:count // 2 * 2:2], mixed[1:count // 2 * 2:2]
    room = jnp.minimum(sizes[source_of] - 1, most - sizes[taker]) // 2
    room = jnp.where((source_of == order[0]) | (taker == order[0]) | (sizes[taker] == 0), 0, jnp.maximum(room, 0))
    moved = jax.random.randint(jax.random.fold_in(own, 4), (count // 2,), 0, 1 << 20) % (room + 1)
    sizes = sizes.at[source_of].add(-moved).at[taker].add(moved)
    items = jnp.searchsorted(jnp.cumsum(sizes), jnp.arange(rows * top), side="right").astype(jnp.int32)
    table = items.reshape(top, rows).T
    table = table[jax.random.permutation(jax.random.fold_in(own, 1), rows)]
    offset_by = jax.random.randint(jax.random.fold_in(own, 2), (rows, 1), 0, top)
    return jnp.take_along_axis(table, (jnp.arange(top)[None, :] + offset_by) % top, axis=1)


def load_shares(count, total, reach, lean, full):
    portions = [(1 << 20) // math.isqrt(grade ** lean) + 1 for grade in range(1, count + 1)]
    largest = reach if full else min(reach, max(-(-total // count), total * portions[0] // sum(portions)))
    least = 1 if total - largest >= count - 1 else 0
    given, rest = [largest] + [least] * (count - 1), total - largest - least * (count - 1)
    while rest > 0:
        candidates = [i for i in range(1, count) if given[i] < largest] or [i for i in range(1, count) if given[i] < reach]
        mass, remaining = sum([portions[i] for i in candidates]), rest
        for i in candidates:
            addition = min(reach - given[i], max(1, remaining * portions[i] // mass), rest)
            given[i] = given[i] + addition
            rest = rest - addition
    return np.array(given)


def gaussian(key, shape, scale, reach, shards=(), held_as=jnp.bfloat16):
    array = jax.random.normal(key, shape, jnp.float32) * scale
    if len(shards) > 0:
        array = level_of(key, shape, shards, -0.22, 0.18) * array
    return jnp.clip(array, min=-reach, max=reach).astype(held_as)


def setup_inputs(seed: int = 0, part: int = 0) -> dict:
    keys = jax.random.split(jax.random.key(seed), 10)
    part_splits = jax.random.split(jax.random.fold_in(keys[9], part), 10)
    tokens = gaussian(part_splits[0], (TOKENS, D), 1.0, 6.0, ((0, 16),))
    expert_ids_keys = jax.random.split(jax.random.fold_in(part_splits[1], 1), TOKENS // ROWS)
    expert_ids_turns = jax.random.permutation(jax.random.fold_in(part_splits[1], 3), TOKENS // ROWS)
    expert_ids = jax.vmap(lambda own, number: shared_out(jax.random.fold_in(part_splits[1], 2), own, number, ROWS, EXPERTS, TOPK, CAP, 2))(expert_ids_keys, expert_ids_turns).reshape((TOKENS, TOPK))
    combine_weights = jnp.clip(jnp.exp(math.log(1.0) - 2.306499 * jax.random.uniform(part_splits[2], (TOKENS, TOPK), jnp.float32) ** level_of(part_splits[2], (TOKENS, TOPK), ((0, 16),), -0.2, 0.2)), 0.099609375, 1.0).astype(jnp.bfloat16)
    expert_weight = gaussian(keys[3], (EXPERTS, D, H), D ** -0.5, 0.09375, ((0, 16),))
    query_latent = draw_query_latent(jax.random.fold_in(jax.random.fold_in(keys[9], part), 71), part)
    query_rope = draw_query_rope(jax.random.fold_in(jax.random.fold_in(keys[9], part), 71), part)
    cache_latent = draw_cache_latent(jax.random.fold_in(jax.random.fold_in(keys[9], part), 71), part)
    cache_rope = draw_cache_rope(jax.random.fold_in(jax.random.fold_in(keys[9], part), 71), part)
    lengths = draw_lengths(jax.random.fold_in(jax.random.fold_in(keys[9], part), 71), part)
    return {"tokens": tokens, "expert_ids": expert_ids, "combine_weights": combine_weights, "expert_weight": expert_weight, "query_latent": query_latent, "query_rope": query_rope, "cache_latent": cache_latent, "cache_rope": cache_rope, "lengths": lengths}


score_scale = 192.0 ** -0.5


def slot_tables(picked, weights, experts, capacity):
    row_count, choose = picked.shape
    flat_picks = picked.reshape(-1)
    matches = (flat_picks[:, None] == jnp.arange(experts, dtype=jnp.int32)[None, :]).astype(jnp.int32)
    earlier = jnp.cumsum(matches, axis=0) - matches
    position = jnp.sum(earlier * matches, axis=1).astype(jnp.int32)
    slot_index = flat_picks * capacity + position
    slot_hits = (slot_index[:, None] == jnp.arange(experts * capacity, dtype=jnp.int32)[None, :]).astype(jnp.float32)
    owner = (jnp.arange(row_count * choose, dtype=jnp.int32)[:, None] // choose == jnp.arange(row_count, dtype=jnp.int32)[None, :]).astype(jnp.float32)
    dispatch = jnp.dot(slot_hits.T, owner, precision=lax.Precision.HIGHEST)
    combine = jnp.dot(owner.T, slot_hits * weights.astype(jnp.float32).reshape(-1)[:, None], precision=lax.Precision.HIGHEST)
    return dispatch, combine


def reference(tokens, expert_ids, combine_weights, expert_weight, query_latent, query_rope, cache_latent, cache_rope, lengths):
    devices = N_NODE * N_LOCAL * N_PAIR
    token_blocks = tokens.reshape(devices, ROWS, D)
    id_blocks = expert_ids.reshape(devices, ROWS, TOPK)
    weight_blocks = combine_weights.reshape(devices, ROWS, TOPK)

    def build(block):
        picked, weights, block_rows = block
        dispatch, combine = slot_tables(picked, weights, EXPERTS, CAP)
        outgoing = jnp.dot(dispatch, block_rows.astype(jnp.float32), precision=lax.Precision.HIGHEST).astype(jnp.bfloat16)
        return outgoing, combine

    outgoing, combine = lax.map(build, (id_blocks, weight_blocks, token_blocks))
    by_expert = jnp.swapaxes(outgoing.reshape(devices, EXPERTS, CAP, D), 0, 1).reshape(EXPERTS, devices * CAP, D)

    def serve(item):
        rows_in, matrix = item
        return jax.nn.silu(jnp.dot(rows_in, matrix, preferred_element_type=jnp.float32)).astype(jnp.bfloat16)

    served = lax.map(serve, (by_expert, expert_weight))
    returned = jnp.swapaxes(served.reshape(EXPERTS, devices, CAP, H), 0, 1).reshape(devices, EXPERTS * CAP, H)

    def blend(item):
        table, values = item
        return jnp.dot(table, values.astype(jnp.float32), precision=lax.Precision.HIGHEST)

    expert_mix = lax.map(blend, (combine, returned)).reshape(TOKENS, H).astype(jnp.bfloat16)

    rotary = query_rope.reshape(TOKENS, HEADS, ROPE).astype(jnp.float32)
    scores = jnp.einsum('rhc,rlc->rhl', query_latent.astype(jnp.float32), cache_latent.astype(jnp.float32))
    scores = scores + jnp.einsum('rhc,rcl->rhl', rotary, cache_rope.astype(jnp.float32))
    scores = scores * score_scale
    visible = jnp.arange(LMAX, dtype=jnp.int32)[None, None, :] < lengths[:, None, None]
    scores = jnp.where(visible, scores, -1e30)
    highest = jnp.max(scores, axis=2, keepdims=True)
    exponent = jnp.exp(scores - highest)
    weights_bf = (exponent / jnp.sum(exponent, axis=2, keepdims=True)).astype(jnp.bfloat16)
    attended = jnp.einsum('rhl,rlc->rhc', weights_bf.astype(jnp.float32), cache_latent.astype(jnp.float32)).astype(jnp.bfloat16)
    return expert_mix, attended
```

```python
import functools

import jax
import jax.numpy as jnp
from jax import lax
from jax.experimental import pallas as pl
from jax.experimental.pallas import tpu as pltpu
from jax.sharding import PartitionSpec as P

score_scale = 192.0 ** (-0.5)
EXPERT_AXES = ("node", "local", "pair")
LANES = 128


def slot_tables(picked, weights, experts, capacity):
    row_count, choose = picked.shape
    flat_picks = picked.reshape(-1)
    matches = (flat_picks[:, None] == jnp.arange(experts, dtype=jnp.int32)[None, :]).astype(
        jnp.int32
    )
    earlier = jnp.cumsum(matches, axis=0) - matches
    position = jnp.sum(earlier * matches, axis=1)
    slot_index = flat_picks * capacity + position
    slot_hits = (
        slot_index[:, None] == jnp.arange(experts * capacity, dtype=jnp.int32)[None, :]
    ).astype(jnp.float32)
    owner = (
        jnp.arange(row_count * choose, dtype=jnp.int32)[:, None] // choose
        == jnp.arange(row_count, dtype=jnp.int32)[None, :]
    ).astype(jnp.float32)
    dispatch = jnp.dot(slot_hits.T, owner, precision=lax.Precision.HIGHEST)
    combine = jnp.dot(
        owner.T,
        slot_hits * weights.astype(jnp.float32).reshape(-1)[:, None],
        precision=lax.Precision.HIGHEST,
    )
    return (dispatch, combine)


def attend_kernel(lengths_ref, ql_ref, qr_ref, cl_ref, cr_ref, out_ref):
    rows, heads, _ = ql_ref.shape
    context = cr_ref.shape[2]
    first = pl.program_id(0) * rows
    place = lax.broadcasted_iota(jnp.int32, (heads, context), 1)
    for r in range(rows):
        cached = cl_ref[r]
        scores = lax.dot_general(
            ql_ref[r], cached, (((1,), (1,)), ((), ())), preferred_element_type=jnp.float32
        )
        scores = scores + jnp.dot(qr_ref[r], cr_ref[r], preferred_element_type=jnp.float32)
        scores = jnp.where(place < lengths_ref[first + r], scores * score_scale, -1e30)
        exponent = jnp.exp(scores - jnp.max(scores, axis=1, keepdims=True))
        probs = (exponent / jnp.sum(exponent, axis=1, keepdims=True)).astype(jnp.bfloat16)
        out_ref[r] = jnp.dot(probs, cached, preferred_element_type=jnp.float32).astype(
            out_ref.dtype
        )


def attend(query_latent, query_rope, cache_latent, cache_rope, lengths):
    row_count, heads, latent = query_latent.shape
    rope, context = cache_rope.shape[1:]
    rotary = query_rope.reshape(row_count, heads, rope)
    step = 4 if row_count % 4 == 0 else 1

    def block(*tail):
        return pl.BlockSpec((step,) + tail, lambda i, lengths_ref: (i, 0, 0))

    flops = 2 * row_count * heads * context * (2 * latent + rope)
    return pl.pallas_call(
        attend_kernel,
        out_shape=jax.ShapeDtypeStruct((row_count, heads, latent), jnp.bfloat16),
        grid_spec=pltpu.PrefetchScalarGridSpec(
            num_scalar_prefetch=1,
            grid=(row_count // step,),
            in_specs=[
                block(heads, latent),
                block(heads, rope),
                block(context, latent),
                block(rope, context),
            ],
            out_specs=block(heads, latent),
        ),
        compiler_params=pltpu.CompilerParams(vmem_limit_bytes=24 * 2**20),
        cost_estimate=pl.CostEstimate(
            flops=flops,
            bytes_accessed=2 * row_count * (latent * (2 * heads + context) + rope * (heads + context)),
            transcendentals=row_count * heads * context,
        ),
    )(lengths, query_latent, rotary, cache_latent, cache_rope)


def expert_by_slots(tokens, expert_ids, combine_weights, expert_weight):
    row_count, model_width = tokens.shape
    choose = expert_ids.shape[1]
    experts = lax.axis_size(EXPERT_AXES)
    capacity = min(row_count, 3 * max(1, (row_count * choose + experts - 1) // experts))
    matrix = expert_weight[0]
    dispatch, combine = slot_tables(expert_ids, combine_weights, experts, capacity)
    outgoing = jnp.dot(
        dispatch.astype(jnp.bfloat16), tokens, preferred_element_type=jnp.float32
    ).astype(jnp.bfloat16)
    outgoing = outgoing.reshape(experts, capacity, model_width)
    received = lax.all_to_all(outgoing, EXPERT_AXES, split_axis=0, concat_axis=0, tiled=True)
    hidden = jnp.dot(received.reshape(-1, model_width), matrix, preferred_element_type=jnp.float32)
    returned = lax.all_to_all(
        jax.nn.silu(hidden).astype(jnp.bfloat16).reshape(received.shape[:-1] + (matrix.shape[1],)),
        EXPERT_AXES,
        split_axis=0,
        concat_axis=0,
        tiled=True,
    )
    returned = returned.reshape(experts * capacity, -1).astype(jnp.float32)
    mixture = jnp.dot(combine, returned, precision=lax.Precision.HIGHEST)
    return mixture.astype(jnp.bfloat16)


def payload_kernel(ids_ref, weights_ref, tokens_ref, out_ref):
    choose, rows = ids_ref.shape
    width = tokens_ref.shape[1]
    expert = lax.broadcasted_iota(jnp.int32, (LANES, rows), 0)
    table = jnp.zeros((LANES, rows), jnp.float32)
    for k in range(choose):
        table = table + jnp.where(
            expert == ids_ref[pl.ds(k, 1), :], weights_ref[pl.ds(k, 1), :].astype(jnp.float32), 0.0
        )
    eye = (
        lax.broadcasted_iota(jnp.int32, (rows, rows), 0)
        == lax.broadcasted_iota(jnp.int32, (rows, rows), 1)
    ).astype(jnp.bfloat16)
    out_ref[:, :width] = tokens_ref[...]
    out_ref[:, width:] = lax.dot_general(
        eye,
        table.astype(jnp.bfloat16),
        (((1,), (1,)), ((), ())),
        preferred_element_type=jnp.float32,
    ).astype(jnp.bfloat16)


def make_payload(tokens, expert_ids, combine_weights):
    rows, width = tokens.shape
    return pl.pallas_call(
        payload_kernel,
        out_shape=jax.ShapeDtypeStruct((rows, width + LANES), jnp.bfloat16),
        compiler_params=pltpu.CompilerParams(vmem_limit_bytes=4 * 2**20),
        cost_estimate=pl.CostEstimate(
            flops=0, bytes_accessed=4 * rows * width, transcendentals=0
        ),
    )(expert_ids.T, combine_weights.T, tokens)


def expert_kernel(count, scalar_ref, *refs):
    blocks, (own_ref, other_ref), outs = refs[:count], refs[count : count + 2], refs[count + 2 :]
    rows = jnp.concatenate([block[...] for block in blocks], axis=0) if count > 1 else blocks[0][...]
    width = own_ref.shape[0]
    features, shares = rows[:, :width], rows[:, width:].astype(jnp.float32)
    lane = lax.broadcasted_iota(jnp.int32, shares.shape, 1)
    total = None
    for which, matrix_ref in ((0, own_ref), (1, other_ref)):
        share = jnp.sum(jnp.where(lane == scalar_ref[which], shares, 0.0), axis=1, keepdims=True)
        hidden = jnp.dot(features, matrix_ref[...], preferred_element_type=jnp.float32)
        term = share * (hidden / (1.0 + jnp.exp(-hidden)))
        total = term if total is None else total + term
    total = total.astype(jnp.bfloat16)
    step = blocks[0].shape[0]
    for i, out_ref in enumerate(outs):
        out_ref[...] = total[i * step : (i + 1) * step]


def serve(blocks, own, other, experts_here):
    count = len(blocks)
    rows, padded = blocks[0].shape
    width, hidden = own.shape
    tile = 256
    weight_spec = pl.BlockSpec((width, tile), lambda n, s: (0, n))
    return pl.pallas_call(
        functools.partial(expert_kernel, count),
        out_shape=[jax.ShapeDtypeStruct((rows, hidden), jnp.bfloat16)] * count,
        grid_spec=pltpu.PrefetchScalarGridSpec(
            num_scalar_prefetch=1,
            grid=(hidden // tile,),
            in_specs=[pl.BlockSpec((rows, padded), lambda n, s: (0, 0))] * count
            + [weight_spec, weight_spec],
            out_specs=[pl.BlockSpec((rows, tile), lambda n, s: (0, n))] * count,
        ),
        compiler_params=pltpu.CompilerParams(vmem_limit_bytes=24 * 2**20),
        cost_estimate=pl.CostEstimate(
            flops=4 * count * rows * width * hidden,
            bytes_accessed=4 * width * hidden,
            transcendentals=2 * count * rows * hidden,
        ),
    )(experts_here, *blocks, own, other)


def swap(value, axis, size, mask):
    return lax.ppermute(value, axis, [(i, i ^ mask) for i in range(size)])


def expert_by_gather(tokens, expert_ids, combine_weights, expert_weight):
    nodes, locals_, pairs = (lax.axis_size(axis) for axis in EXPERT_AXES)
    own = expert_weight[0]
    other = swap(own, "pair", pairs, 1)
    here = lax.axis_index(EXPERT_AXES).astype(jnp.int32)
    experts_here = jnp.stack([here, here ^ 1])

    mine = make_payload(tokens, expert_ids, combine_weights)
    near = {0: mine}
    for n in range(nodes - 1, 0, -1):
        near[n] = swap(mine, "node", nodes, n)
    names = [(n, l) for l in range(locals_) for n in range(nodes)]
    blocks = [
        near[n] if l == 0 else swap(near[n], ("local"), locals_, l) for n, l in names
    ]
    parts = dict(zip(names, serve(blocks, own, other, experts_here)))
    total = parts[(0, 0)].astype(jnp.float32)
    for n, l in names[1:]:
        came = swap(parts[(n, l)], ("node", "local"), nodes * locals_, n * locals_ + l)
        total = total + came.astype(jnp.float32)
    return total.astype(jnp.bfloat16)


def expert_part(tokens, expert_ids, combine_weights, expert_weight):
    sizes = tuple(lax.axis_size(axis) for axis in EXPERT_AXES)
    rows, choose = tokens.shape[0], expert_ids.shape[1]
    experts = lax.axis_size(EXPERT_AXES)
    if sizes == (4, 2, 2) and rows * choose * 2 >= rows * experts and experts <= LANES:
        return expert_by_gather(tokens, expert_ids, combine_weights, expert_weight)
    return expert_by_slots(tokens, expert_ids, combine_weights, expert_weight)


def body(
    tokens,
    expert_ids,
    combine_weights,
    expert_weight,
    query_latent,
    query_rope,
    cache_latent,
    cache_rope,
    lengths,
):
    attended = attend(query_latent, query_rope, cache_latent, cache_rope, lengths)
    expert_mix = expert_part(tokens, expert_ids, combine_weights, expert_weight)
    return (expert_mix, attended)


def solution(mesh):
    rows = ("group",) + EXPERT_AXES
    return jax.shard_map(
        body,
        mesh=mesh,
        in_specs=(
            P(rows, None),
            P(rows, None),
            P(rows, None),
            P(EXPERT_AXES, None, None),
            P(rows, None, None),
            P(rows, None),
            P(rows, None, None),
            P(rows, None, None),
            P(rows),
        ),
        out_specs=(P(rows, None), P(rows, None, None)),
        check_vma=False,
    )
```

```python
import functools

import jax
import jax.numpy as jnp
from jax import lax
from jax.experimental import pallas as pl
from jax.experimental.pallas import tpu as pltpu
from jax.sharding import PartitionSpec as P

score_scale = 192.0 ** (-0.5)
EXPERT_AXES = ("node", "local", "pair")
LANES = 128
VMEM_LIMIT = 16 * 2**20


def slot_tables(picked, weights, experts, capacity):
    row_count, choose = picked.shape
    flat_picks = picked.reshape(-1)
    matches = (flat_picks[:, None] == jnp.arange(experts, dtype=jnp.int32)[None, :]).astype(
        jnp.int32
    )
    earlier = jnp.cumsum(matches, axis=0) - matches
    position = jnp.sum(earlier * matches, axis=1)
    slot_index = flat_picks * capacity + position
    slot_hits = (
        slot_index[:, None] == jnp.arange(experts * capacity, dtype=jnp.int32)[None, :]
    ).astype(jnp.float32)
    owner = (
        jnp.arange(row_count * choose, dtype=jnp.int32)[:, None] // choose
        == jnp.arange(row_count, dtype=jnp.int32)[None, :]
    ).astype(jnp.float32)
    dispatch = jnp.dot(slot_hits.T, owner, precision=lax.Precision.HIGHEST)
    combine = jnp.dot(
        owner.T,
        slot_hits * weights.astype(jnp.float32).reshape(-1)[:, None],
        precision=lax.Precision.HIGHEST,
    )
    return (dispatch, combine)


def attend_kernel(first, loads, lengths_ref, ql_ref, qr_ref, cl_ref, cr_ref, *refs):
    if loads:
        matrix_hbm, out_ref, matrix_ref, sem = refs
        copy = pltpu.make_async_copy(matrix_hbm, matrix_ref, sem)

        @pl.when(pl.program_id(0) == 0)
        def _():
            copy.start()

    else:
        out_ref = refs[-1]
    rows, heads, _ = ql_ref.shape
    context = cr_ref.shape[2]
    start = first + pl.program_id(0) * rows
    place = lax.broadcasted_iota(jnp.int32, (heads, context), 1)
    scores = []
    for r in range(rows):
        s = lax.dot_general(
            ql_ref[r], cl_ref[r], (((1,), (1,)), ((), ())), preferred_element_type=jnp.float32
        )
        s = s + jnp.dot(qr_ref[r], cr_ref[r], preferred_element_type=jnp.float32)
        scores.append(jnp.where(place < lengths_ref[start + r], s * score_scale, -1e30))
    probs = []
    for s in scores:
        exponent = jnp.exp(s - jnp.max(s, axis=1, keepdims=True))
        probs.append((exponent / jnp.sum(exponent, axis=1, keepdims=True)).astype(jnp.bfloat16))
    for r in range(rows):
        out_ref[r] = jnp.dot(probs[r], cl_ref[r], preferred_element_type=jnp.float32).astype(
            out_ref.dtype
        )
    if loads:

        @pl.when(pl.program_id(0) == pl.num_programs(0) - 1)
        def _():
            copy.wait()


def attend_rows(
    first, count, query_latent, rotary, cache_latent, cache_rope, lengths, so_far=None, matrix=None
):
    row_count, heads, latent = query_latent.shape
    rope, context = cache_rope.shape[1:]
    step = 8 if count % 8 == 0 and first % 8 == 0 else 1

    def block(*tail):
        return pl.BlockSpec((step,) + tail, lambda i, lengths_ref: (first // step + i, 0, 0))

    loads = matrix is not None
    extra = [so_far] if so_far is not None else [in_hbm(matrix)] if loads else []
    out_shape = jax.ShapeDtypeStruct((row_count, heads, latent), jnp.bfloat16)
    out_spec = block(heads, latent)
    if loads:
        out_shape = [out_shape, pltpu.VMEM(matrix.shape, matrix.dtype)]
        out_spec = [out_spec, pl.BlockSpec(memory_space=pltpu.VMEM)]
    return pl.pallas_call(
        functools.partial(attend_kernel, first, loads),
        out_shape=out_shape,
        grid_spec=pltpu.PrefetchScalarGridSpec(
            num_scalar_prefetch=1,
            grid=(count // step,),
            in_specs=[
                block(heads, latent),
                block(heads, rope),
                block(context, latent),
                block(rope, context),
            ]
            + [pl.BlockSpec(memory_space=pl.ANY)] * len(extra),
            out_specs=out_spec,
            scratch_shapes=[pltpu.SemaphoreType.DMA] if loads else [],
        ),
        input_output_aliases={5: 0} if so_far is not None else {},
        compiler_params=pltpu.CompilerParams(vmem_limit_bytes=12 * 2**20),
    )(lengths, in_hbm(query_latent), rotary, in_hbm(cache_latent), in_hbm(cache_rope), *extra)


def in_hbm(value):
    return pltpu.with_memory_space_constraint(value, pltpu.HBM)


def in_vmem(value):
    return pltpu.with_memory_space_constraint(value, pltpu.VMEM)


def expert_by_slots(tokens, expert_ids, combine_weights, expert_weight):
    row_count, model_width = tokens.shape
    choose = expert_ids.shape[1]
    experts = lax.axis_size(EXPERT_AXES)
    capacity = min(row_count, 3 * max(1, (row_count * choose + experts - 1) // experts))
    matrix = expert_weight[0]
    dispatch, combine = slot_tables(expert_ids, combine_weights, experts, capacity)
    outgoing = jnp.dot(
        dispatch.astype(jnp.bfloat16), tokens, preferred_element_type=jnp.float32
    ).astype(jnp.bfloat16)
    outgoing = outgoing.reshape(experts, capacity, model_width)
    received = lax.all_to_all(outgoing, EXPERT_AXES, split_axis=0, concat_axis=0, tiled=True)
    hidden = jnp.dot(received.reshape(-1, model_width), matrix, preferred_element_type=jnp.float32)
    returned = lax.all_to_all(
        jax.nn.silu(hidden).astype(jnp.bfloat16).reshape(received.shape[:-1] + (matrix.shape[1],)),
        EXPERT_AXES,
        split_axis=0,
        concat_axis=0,
        tiled=True,
    )
    returned = returned.reshape(experts * capacity, -1).astype(jnp.float32)
    mixture = jnp.dot(combine, returned, precision=lax.Precision.HIGHEST)
    return mixture.astype(jnp.bfloat16)


def payload_kernel(
    ids_hbm, weights_hbm, tokens_hbm, rope_hbm, out_ref, rope_ref, ids_ref, weights_ref, sems
):
    choose, rows = ids_ref.shape
    width = tokens_hbm.shape[1]
    copies = [
        pltpu.make_async_copy(ids_hbm, ids_ref, sems.at[0]),
        pltpu.make_async_copy(weights_hbm, weights_ref, sems.at[1]),
        pltpu.make_async_copy(tokens_hbm, out_ref.at[:, pl.ds(0, width)], sems.at[2]),
        pltpu.make_async_copy(rope_hbm, rope_ref, sems.at[3]),
    ]
    for copy in copies:
        copy.start()
    copies[0].wait()
    copies[1].wait()
    expert = lax.broadcasted_iota(jnp.int32, (LANES, rows), 0)
    table = jnp.zeros((LANES, rows), jnp.float32)
    ids, weights = ids_ref[...], weights_ref[...].astype(jnp.float32)
    for k in range(choose):
        table = table + jnp.where(expert == ids[k : k + 1], weights[k : k + 1], 0.0)
    eye = (
        lax.broadcasted_iota(jnp.int32, (rows, rows), 0)
        == lax.broadcasted_iota(jnp.int32, (rows, rows), 1)
    ).astype(jnp.bfloat16)
    out_ref[:, width:] = lax.dot_general(
        eye,
        table.astype(jnp.bfloat16),
        (((1,), (1,)), ((), ())),
        preferred_element_type=jnp.float32,
    ).astype(jnp.bfloat16)
    copies[2].wait()
    copies[3].wait()


def make_payload(tokens, expert_ids, combine_weights, query_rope):
    rows, width = tokens.shape
    choose = expert_ids.shape[1]
    return pl.pallas_call(
        payload_kernel,
        out_shape=[
            pltpu.VMEM((rows, width + LANES), jnp.bfloat16),
            pltpu.VMEM(query_rope.shape, query_rope.dtype),
        ],
        in_specs=[pl.BlockSpec(memory_space=pl.ANY)] * 4,
        out_specs=[pl.BlockSpec(memory_space=pltpu.VMEM)] * 2,
        scratch_shapes=[
            pltpu.VMEM((choose, rows), jnp.int32),
            pltpu.VMEM((choose, rows), jnp.bfloat16),
            pltpu.SemaphoreType.DMA((4,)),
        ],
        compiler_params=pltpu.CompilerParams(vmem_limit_bytes=4 * 2**20),
        cost_estimate=pl.CostEstimate(
            flops=0, bytes_accessed=4 * rows * width, transcendentals=0
        ),
    )(in_hbm(expert_ids.T), in_hbm(combine_weights.T), in_hbm(tokens), in_hbm(query_rope))


def expert_kernel(count, *refs):
    here = lax.axis_index(EXPERT_AXES).astype(jnp.int32)
    blocks, (own_ref, other_hbm) = refs[:count], refs[count : count + 2]
    near_ref, far_ref, other_ref, sems = refs[count + 2 :]
    width, hidden = own_ref.shape
    tile = 256
    copies = [
        pltpu.make_async_copy(
            other_hbm.at[:, pl.ds(n, tile)], other_ref.at[:, pl.ds(n, tile)], sems.at[n // tile]
        )
        for n in range(0, hidden, tile)
    ]
    for copy in copies:
        copy.start()
    rows = jnp.concatenate([block[...] for block in blocks], axis=0)
    features, shares = rows[:, :width], rows[:, width:].astype(jnp.float32)
    lane = lax.broadcasted_iota(jnp.int32, shares.shape, 1)
    share = [
        jnp.sum(jnp.where(lane == (here ^ which), shares, 0.0), axis=1, keepdims=True)
        for which in range(2)
    ]

    def term(which, matrix_ref, n):
        value = jnp.dot(features, matrix_ref[:, n : n + tile], preferred_element_type=jnp.float32)
        return share[which] * (value / (1.0 + jnp.exp(-value)))

    half = near_ref.shape[0]
    firsts = [term(0, own_ref, n) for n in range(0, hidden, tile)]
    for n, copy, first in zip(range(0, hidden, tile), copies, firsts):
        copy.wait()
        total = first + term(1, other_ref, n)
        near_ref[:, n : n + tile] = total[:half]
        far_ref[:, n : n + tile] = total[half:].astype(jnp.bfloat16)


def serve(blocks, own, other):
    count = len(blocks)
    rows = blocks[0].shape[0]
    width, hidden = own.shape
    whole = pl.BlockSpec(memory_space=pltpu.VMEM)
    half = count // 2 * rows
    return pl.pallas_call(
        functools.partial(expert_kernel, count),
        out_shape=[
            pltpu.VMEM((half, hidden), jnp.float32),
            pltpu.VMEM((half, hidden), jnp.bfloat16),
        ],
        in_specs=[whole] * (count + 1) + [pl.BlockSpec(memory_space=pl.ANY)],
        out_specs=[whole] * 2,
        scratch_shapes=[
            pltpu.VMEM((width, hidden), jnp.bfloat16),
            pltpu.SemaphoreType.DMA((hidden // 256,)),
        ],
        compiler_params=pltpu.CompilerParams(vmem_limit_bytes=VMEM_LIMIT),
        cost_estimate=pl.CostEstimate(
            flops=4 * count * rows * width * hidden,
            bytes_accessed=4 * width * hidden,
            transcendentals=2 * count * rows * hidden,
        ),
    )(*map(in_vmem, blocks), in_vmem(own), in_hbm(other))


def swap(value, axis, size, mask):
    return lax.ppermute(value, axis, [(i, i ^ mask) for i in range(size)])


def tie(value, *others):
    return lax.optimization_barrier((value,) + others)[0]


def gathered(attention, tokens, expert_ids, combine_weights, expert_weight):
    nodes, locals_, pairs = (lax.axis_size(axis) for axis in EXPERT_AXES)
    rows = tokens.shape[0]
    own = expert_weight[0]
    other = swap(own, "pair", pairs, 1)

    query_latent, query_rope, cache_latent, cache_rope, lengths = attention
    mine, query_rope = make_payload(tokens, expert_ids, combine_weights, query_rope)
    near = {0: mine}
    for n in range(nodes - 1, 0, -1):
        near[n] = swap(mine, "node", nodes, n)
    far = {}
    far[0] = swap(mine, "local", locals_, 1)
    far[1] = swap(mine, ("node", "local"), nodes * locals_, locals_ + 1)
    count, heads, _ = query_latent.shape
    half = count // 2
    rotary = query_rope.reshape(count, heads, cache_rope.shape[1])
    rest = (rotary, cache_latent, cache_rope, lengths)
    attended, own = attend_rows(0, half, tie(query_latent, mine), *rest, matrix=own)
    far[3] = swap(tie(near[3], attended), "local", locals_, 1)
    far[2] = swap(tie(near[2], attended), "local", locals_, 1)

    blocks = [near[n] for n in range(nodes)] + [far[n] for n in range(nodes)]
    kept, sent = serve(blocks, own, other)
    came = swap(sent, "local", locals_, 1)
    attended = attend_rows(half, count - half, tie(query_latent, sent), *rest, attended)
    came = tie(came, attended)
    kept = kept.reshape(nodes, rows, -1)
    came = came.reshape(nodes, rows, -1)
    total = kept[0] + came[0].astype(jnp.float32)
    for n in range(nodes - 1, 0, -1):
        part = (kept[n] + came[n].astype(jnp.float32)).astype(jnp.bfloat16)
        total = total + swap(part, "node", nodes, n).astype(jnp.float32)
    return total.astype(jnp.bfloat16), attended


def body(
    tokens,
    expert_ids,
    combine_weights,
    expert_weight,
    query_latent,
    query_rope,
    cache_latent,
    cache_rope,
    lengths,
):
    sizes = tuple(lax.axis_size(axis) for axis in EXPERT_AXES)
    attention = (query_latent, query_rope, cache_latent, cache_rope, lengths)
    if sizes == (4, 2, 2):
        return gathered(attention, tokens, expert_ids, combine_weights, expert_weight)
    count, heads, _ = query_latent.shape
    rotary = query_rope.reshape(count, heads, cache_rope.shape[1])
    attended = attend_rows(0, count, query_latent, rotary, cache_latent, cache_rope, lengths)
    expert_mix = expert_by_slots(tokens, expert_ids, combine_weights, expert_weight)
    return (expert_mix, attended)


def solution(mesh):
    rows = ("group",) + EXPERT_AXES
    return jax.shard_map(
        body,
        mesh=mesh,
        in_specs=(
            P(rows, None),
            P(rows, None),
            P(rows, None),
            P(EXPERT_AXES, None, None),
            P(rows, None, None),
            P(rows, None),
            P(rows, None, None),
            P(rows, None, None),
            P(rows),
        ),
        out_specs=(P(rows, None), P(rows, None, None)),
        check_vma=False,
    )
```

```python
import functools

import jax
import jax.numpy as jnp
from jax import lax
from jax.experimental import pallas as pl
from jax.experimental.pallas import tpu as pltpu
from jax.sharding import PartitionSpec as P

score_scale = 192.0 ** (-0.5)
EXPERT_AXES = ("node", "local", "pair")
LANES = 128
VMEM_LIMIT = 8 * 2**20


def slot_tables(picked, weights, experts, capacity):
    row_count, choose = picked.shape
    flat_picks = picked.reshape(-1)
    matches = (flat_picks[:, None] == jnp.arange(experts, dtype=jnp.int32)[None, :]).astype(
        jnp.int32
    )
    earlier = jnp.cumsum(matches, axis=0) - matches
    position = jnp.sum(earlier * matches, axis=1)
    slot_index = flat_picks * capacity + position
    slot_hits = (
        slot_index[:, None] == jnp.arange(experts * capacity, dtype=jnp.int32)[None, :]
    ).astype(jnp.float32)
    owner = (
        jnp.arange(row_count * choose, dtype=jnp.int32)[:, None] // choose
        == jnp.arange(row_count, dtype=jnp.int32)[None, :]
    ).astype(jnp.float32)
    dispatch = jnp.dot(slot_hits.T, owner, precision=lax.Precision.HIGHEST)
    combine = jnp.dot(
        owner.T,
        slot_hits * weights.astype(jnp.float32).reshape(-1)[:, None],
        precision=lax.Precision.HIGHEST,
    )
    return (dispatch, combine)


def attend_core(first, limits, ql_ref, qr_ref, cl_ref, cr_ref, out_ref, pairs_ref, rotary_ref):
    rows, heads, _ = ql_ref.shape
    rope, context = cr_ref.shape[1:]
    all_rows, width = qr_ref.shape
    place = lax.broadcasted_iota(jnp.int32, (heads, context), 1)
    pairs = width // (2 * rope)
    for p in range(pairs):
        pairs_ref[pl.ds(p * all_rows, all_rows), :] = qr_ref[
            :, p * 2 * rope : (p + 1) * 2 * rope
        ].astype(jnp.float32)
    for r in range(rows):
        both = pairs_ref[pl.ds(first + r, pairs, stride=all_rows), :].astype(jnp.bfloat16)
        for odd in range(2):
            rotary_ref[r, pl.ds(odd, pairs, stride=2), :] = jnp.dot(
                both[:, odd * rope : (odd + 1) * rope],
                cr_ref[r],
                preferred_element_type=jnp.float32,
            )
    scores = []
    for r in range(rows):
        s = lax.dot_general(
            ql_ref[r], cl_ref[r], (((1,), (1,)), ((), ())), preferred_element_type=jnp.float32
        )
        s = (s + rotary_ref[r]) * score_scale
        scores.append(jnp.where(place < limits[r], s, -1e30))
    probs = []
    for s in scores:
        exponent = jnp.exp(s - jnp.max(s, axis=1, keepdims=True))
        probs.append((exponent / jnp.sum(exponent, axis=1, keepdims=True)).astype(jnp.bfloat16))
    for r, p in enumerate(probs):
        out_ref[r] = jnp.dot(p, cl_ref[r], preferred_element_type=jnp.float32).astype(
            out_ref.dtype
        )


def fetch(sources, targets, sems):
    copies = [
        pltpu.make_async_copy(source, target, sems.at[i])
        for i, (source, target) in enumerate(zip(sources, targets))
    ]
    for copy in copies:
        copy.start()
    return copies


def attend_kernel(first, lengths_hbm, ql_hbm, qr_hbm, cl_hbm, cr_hbm, out_hbm, *scratch):
    lengths_ref, ql_ref, qr_ref, cl_ref, cr_ref, out_ref, pairs_ref, rotary_ref, sems = scratch
    rows = ql_ref.shape[0]
    part = pl.ds(first, rows)
    sources = (lengths_hbm, qr_hbm, cr_hbm.at[part], cl_hbm.at[part], ql_hbm.at[part])
    for copy in fetch(sources, (lengths_ref, qr_ref, cr_ref, cl_ref, ql_ref), sems):
        copy.wait()
    limits = [lengths_ref[first + r] for r in range(rows)]
    attend_core(first, limits, ql_ref, qr_ref, cl_ref, cr_ref, out_ref, pairs_ref, rotary_ref)
    for copy in fetch((out_ref,), (out_hbm.at[part],), sems):
        copy.wait()


def staged_kernel(first, limits_ref, ql_ref, qr_ref, cl_ref, cr_ref, so_far, out_hbm, *scratch):
    out_ref, pairs_ref, rotary_ref, sems = scratch
    rows = ql_ref.shape[0]
    limits = [limits_ref[pl.ds(r, 1), :] for r in range(rows)]
    attend_core(first, limits, ql_ref, qr_ref, cl_ref, cr_ref, out_ref, pairs_ref, rotary_ref)
    for copy in fetch((out_ref,), (out_hbm.at[pl.ds(first, rows)],), sems):
        copy.wait()


def attend_cost(count, heads, context, latent, rope):
    return pl.CostEstimate(
        flops=2 * count * heads * context * (2 * latent + rope),
        bytes_accessed=10 * count * latent * (2 * heads + context),
        transcendentals=count * heads * context,
    )


ANYWHERE = pl.BlockSpec(memory_space=pl.ANY)
IN_VMEM = pl.BlockSpec(memory_space=pltpu.VMEM)


def attend_rows(first, count, query_latent, query_rope, cache_latent, cache_rope, lengths):
    row_count, heads, latent = query_latent.shape
    rope, context = cache_rope.shape[1:]
    operands = (lengths, query_latent, query_rope, cache_latent, cache_rope)
    return pl.pallas_call(
        functools.partial(attend_kernel, first),
        out_shape=pltpu.HBM((row_count, heads, latent), jnp.bfloat16),
        in_specs=[ANYWHERE] * 5,
        out_specs=ANYWHERE,
        scratch_shapes=[
            pltpu.SMEM(lengths.shape, lengths.dtype),
            pltpu.VMEM((count, heads, latent), jnp.bfloat16),
            pltpu.VMEM(query_rope.shape, jnp.bfloat16),
            pltpu.VMEM((count, context, latent), jnp.bfloat16),
            pltpu.VMEM((count, rope, context), jnp.bfloat16),
            pltpu.VMEM((count, heads, latent), jnp.bfloat16),
            pltpu.VMEM((row_count * heads // 2, 2 * rope), jnp.float32),
            pltpu.VMEM((count, heads, context), jnp.float32),
            pltpu.SemaphoreType.DMA((5,)),
        ],
        compiler_params=pltpu.CompilerParams(vmem_limit_bytes=(count + 4) * 2**20),
        cost_estimate=attend_cost(count, heads, context, latent, rope),
    )(*map(in_hbm, operands))


def attend_staged(first, staged, so_far):
    limits, query_latent, query_rope, cache_latent, cache_rope = staged
    count, heads, latent = query_latent.shape
    rope, context = cache_rope.shape[1:]
    return pl.pallas_call(
        functools.partial(staged_kernel, first),
        out_shape=pltpu.HBM(so_far.shape, so_far.dtype),
        in_specs=[IN_VMEM] * 5 + [ANYWHERE],
        out_specs=ANYWHERE,
        scratch_shapes=[
            pltpu.VMEM((count, heads, latent), jnp.bfloat16),
            pltpu.VMEM((so_far.shape[0] * heads // 2, 2 * rope), jnp.float32),
            pltpu.VMEM((count, heads, context), jnp.float32),
            pltpu.SemaphoreType.DMA((1,)),
        ],
        input_output_aliases={5: 0},
        compiler_params=pltpu.CompilerParams(vmem_limit_bytes=(count + 4) * 2**20),
        cost_estimate=attend_cost(count, heads, context, latent, rope),
    )(*map(in_vmem, staged), so_far)


def stage_kernel(first, matrix_hbm, lengths_hbm, ql_hbm, qr_hbm, cl_hbm, cr_hbm, *refs):
    matrix_ref, limits_ref, ql_ref, qr_ref, cl_ref, cr_ref, lengths_ref, sems = refs
    rows = ql_ref.shape[0]
    part = pl.ds(first, rows)
    pieces = sems.shape[0] - 5
    step = matrix_hbm.shape[0] // pieces
    cuts = [pl.ds(i * step, step) for i in range(pieces)]
    sources = [lengths_hbm, qr_hbm, cr_hbm.at[part], cl_hbm.at[part], ql_hbm.at[part]]
    targets = [lengths_ref, qr_ref, cr_ref, cl_ref, ql_ref]
    copies = fetch(
        sources + [matrix_hbm.at[cut] for cut in cuts],
        targets + [matrix_ref.at[cut] for cut in cuts],
        sems,
    )
    for i, copy in enumerate(copies):
        copy.wait()
        if i == 0:
            for r in range(rows):
                limits_ref[pl.ds(r, 1), :] = jnp.full(
                    (1, limits_ref.shape[1]), lengths_ref[first + r], jnp.int32
                )


def stage(first, count, matrix, query_latent, query_rope, cache_latent, cache_rope, lengths):
    heads, latent = query_latent.shape[1:]
    rope, context = cache_rope.shape[1:]
    operands = (matrix, lengths, query_latent, query_rope, cache_latent, cache_rope)
    out = pl.pallas_call(
        functools.partial(stage_kernel, first),
        out_shape=[
            pltpu.VMEM(matrix.shape, matrix.dtype),
            pltpu.VMEM((count, context), jnp.int32),
            pltpu.VMEM((count, heads, latent), jnp.bfloat16),
            pltpu.VMEM(query_rope.shape, jnp.bfloat16),
            pltpu.VMEM((count, context, latent), jnp.bfloat16),
            pltpu.VMEM((count, rope, context), jnp.bfloat16),
        ],
        in_specs=[ANYWHERE] * 6,
        out_specs=[IN_VMEM] * 6,
        scratch_shapes=[
            pltpu.SMEM(lengths.shape, lengths.dtype),
            pltpu.SemaphoreType.DMA((5 + (4 if matrix.shape[0] % 64 == 0 else 1),)),
        ],
        compiler_params=pltpu.CompilerParams(vmem_limit_bytes=2**20),
        cost_estimate=pl.CostEstimate(
            flops=0, bytes_accessed=2 * matrix.size, transcendentals=0
        ),
    )(*map(in_hbm, operands))
    return out[0], out[1:]


def in_hbm(value):
    return pltpu.with_memory_space_constraint(value, pltpu.HBM)


def in_vmem(value):
    return pltpu.with_memory_space_constraint(value, pltpu.VMEM)


def expert_by_slots(tokens, expert_ids, combine_weights, expert_weight):
    row_count, model_width = tokens.shape
    choose = expert_ids.shape[1]
    experts = lax.axis_size(EXPERT_AXES)
    capacity = min(row_count, 3 * max(1, (row_count * choose + experts - 1) // experts))
    matrix = expert_weight[0]
    dispatch, combine = slot_tables(expert_ids, combine_weights, experts, capacity)
    outgoing = jnp.dot(
        dispatch.astype(jnp.bfloat16), tokens, preferred_element_type=jnp.float32
    ).astype(jnp.bfloat16)
    outgoing = outgoing.reshape(experts, capacity, model_width)
    received = lax.all_to_all(outgoing, EXPERT_AXES, split_axis=0, concat_axis=0, tiled=True)
    hidden = jnp.dot(received.reshape(-1, model_width), matrix, preferred_element_type=jnp.float32)
    returned = lax.all_to_all(
        jax.nn.silu(hidden).astype(jnp.bfloat16).reshape(received.shape[:-1] + (matrix.shape[1],)),
        EXPERT_AXES,
        split_axis=0,
        concat_axis=0,
        tiled=True,
    )
    returned = returned.reshape(experts * capacity, -1).astype(jnp.float32)
    mixture = jnp.dot(combine, returned, precision=lax.Precision.HIGHEST)
    return mixture.astype(jnp.bfloat16)


def payload_kernel(
    ids_hbm, weights_hbm, tokens_hbm, out_ref, ids_ref, weights_ref, sems
):
    choose, rows = ids_ref.shape
    width = tokens_hbm.shape[1]
    copies = [
        pltpu.make_async_copy(ids_hbm, ids_ref, sems.at[0]),
        pltpu.make_async_copy(weights_hbm, weights_ref, sems.at[1]),
        pltpu.make_async_copy(tokens_hbm, out_ref.at[:, pl.ds(0, width)], sems.at[2]),
    ]
    for copy in copies:
        copy.start()
    copies[0].wait()
    copies[1].wait()
    expert = lax.broadcasted_iota(jnp.int32, (LANES, rows), 0)
    table = jnp.zeros((LANES, rows), jnp.float32)
    ids, weights = ids_ref[...], weights_ref[...].astype(jnp.float32)
    for k in range(choose):
        table = table + jnp.where(expert == ids[k : k + 1], weights[k : k + 1], 0.0)
    eye = (
        lax.broadcasted_iota(jnp.int32, (rows, rows), 0)
        == lax.broadcasted_iota(jnp.int32, (rows, rows), 1)
    ).astype(jnp.bfloat16)
    out_ref[:, width:] = lax.dot_general(
        eye,
        table.astype(jnp.bfloat16),
        (((1,), (1,)), ((), ())),
        preferred_element_type=jnp.float32,
    ).astype(jnp.bfloat16)
    copies[2].wait()


def make_payload(tokens, expert_ids, combine_weights):
    rows, width = tokens.shape
    choose = expert_ids.shape[1]
    return pl.pallas_call(
        payload_kernel,
        out_shape=pltpu.VMEM((rows, width + LANES), jnp.bfloat16),
        in_specs=[pl.BlockSpec(memory_space=pl.ANY)] * 3,
        out_specs=pl.BlockSpec(memory_space=pltpu.VMEM),
        scratch_shapes=[
            pltpu.VMEM((choose, rows), jnp.int32),
            pltpu.VMEM((choose, rows), jnp.bfloat16),
            pltpu.SemaphoreType.DMA((3,)),
        ],
        compiler_params=pltpu.CompilerParams(vmem_limit_bytes=4 * 2**20),
        cost_estimate=pl.CostEstimate(
            flops=0, bytes_accessed=4 * rows * width, transcendentals=0
        ),
    )(in_hbm(expert_ids.T), in_hbm(combine_weights.T), in_hbm(tokens))


def expert_kernel(count, *refs):
    here = lax.axis_index(EXPERT_AXES).astype(jnp.int32)
    blocks, matrices = refs[:count], refs[count : count + 2]
    near_ref, far_ref = refs[count + 2 :]
    width, hidden = matrices[0].shape
    rows = jnp.concatenate([block[...] for block in blocks], axis=0)
    features, shares = rows[:, :width], rows[:, width:].astype(jnp.float32)
    lane = lax.broadcasted_iota(jnp.int32, shares.shape, 1)
    share = [
        jnp.sum(jnp.where(lane == (here ^ which), shares, 0.0), axis=1, keepdims=True)
        for which in range(2)
    ]
    half = near_ref.shape[0]
    tile = 256
    for n in range(0, hidden, tile):
        total = None
        for which, matrix_ref in enumerate(matrices):
            value = jnp.dot(
                features, matrix_ref[:, n : n + tile], preferred_element_type=jnp.float32
            )
            term = share[which] * (value / (1.0 + jnp.exp(-value)))
            total = term if total is None else total + term
        near_ref[:, n : n + tile] = total[:half]
        far_ref[:, n : n + tile] = total[half:].astype(jnp.bfloat16)


def serve(blocks, own, other):
    count = len(blocks)
    rows = blocks[0].shape[0]
    width, hidden = own.shape
    whole = pl.BlockSpec(memory_space=pltpu.VMEM)
    half = count // 2 * rows
    return pl.pallas_call(
        functools.partial(expert_kernel, count),
        out_shape=[
            pltpu.VMEM((half, hidden), jnp.float32),
            pltpu.VMEM((half, hidden), jnp.bfloat16),
        ],
        in_specs=[whole] * (count + 2),
        out_specs=[whole] * 2,
        compiler_params=pltpu.CompilerParams(vmem_limit_bytes=VMEM_LIMIT),
        cost_estimate=pl.CostEstimate(
            flops=4 * count * rows * width * hidden,
            bytes_accessed=4 * width * hidden,
            transcendentals=2 * count * rows * hidden,
        ),
    )(*map(in_vmem, blocks), in_vmem(own), in_vmem(other))


def swap(value, axis, size, mask):
    return lax.ppermute(value, axis, [(i, i ^ mask) for i in range(size)])


def tie(value, *others):
    return lax.optimization_barrier((value,) + others)[0]


def gathered(attention, tokens, expert_ids, combine_weights, expert_weight):
    nodes, locals_, pairs = (lax.axis_size(axis) for axis in EXPERT_AXES)
    rows = tokens.shape[0]
    own = expert_weight[0]
    other = swap(own, "pair", pairs, 1)

    query_latent, query_rope, cache_latent, cache_rope, lengths = attention
    mine = make_payload(tokens, expert_ids, combine_weights)
    near, far = {0: mine}, {}
    near[1] = swap(mine, "node", nodes, 1)
    far[0] = swap(mine, "local", locals_, 1)
    near[2] = swap(mine, "node", nodes, 2)
    count = query_latent.shape[0]
    half = count // 2
    rest = (query_rope, cache_latent, cache_rope, lengths)
    attended = attend_rows(0, half, tie(query_latent, mine), *rest)
    near[1], far[0], near[2], _ = lax.optimization_barrier((near[1], far[0], near[2], attended))
    near[3] = swap(near[2], "node", nodes, 1)
    far[2] = swap(near[2], "local", locals_, 1)
    far[1] = swap(far[0], "node", nodes, 1)
    far[3] = swap(near[3], "local", locals_, 1)
    own, staged = stage(half, count - half, tie(own, near[3]), query_latent, *rest)
    far[1], far[2], far[3], _ = lax.optimization_barrier((far[1], far[2], far[3], own))
    blocks = [near[n] for n in range(nodes)] + [far[n] for n in range(nodes)]
    kept, sent = serve(blocks, own, other)
    came = swap(sent, "local", locals_, 1)
    attended = attend_staged(half, staged, tie(attended, sent))
    came = tie(came, attended)
    kept = kept.reshape(nodes, rows, -1)
    came = came.reshape(nodes, rows, -1)
    total = kept[0] + came[0].astype(jnp.float32)
    for n in (2, 1, 3):
        part = (kept[n] + came[n].astype(jnp.float32)).astype(jnp.bfloat16)
        total = total + swap(part, "node", nodes, n).astype(jnp.float32)
    return total.astype(jnp.bfloat16), attended


def body(
    tokens,
    expert_ids,
    combine_weights,
    expert_weight,
    query_latent,
    query_rope,
    cache_latent,
    cache_rope,
    lengths,
):
    sizes = tuple(lax.axis_size(axis) for axis in EXPERT_AXES)
    attention = (query_latent, query_rope, cache_latent, cache_rope, lengths)
    if sizes == (4, 2, 2):
        return gathered(attention, tokens, expert_ids, combine_weights, expert_weight)
    count = query_latent.shape[0]
    attended = attend_rows(0, count, query_latent, query_rope, cache_latent, cache_rope, lengths)
    expert_mix = expert_by_slots(tokens, expert_ids, combine_weights, expert_weight)
    return (expert_mix, attended)


def solution(mesh):
    rows = ("group",) + EXPERT_AXES
    return jax.shard_map(
        body,
        mesh=mesh,
        in_specs=(
            P(rows, None),
            P(rows, None),
            P(rows, None),
            P(EXPERT_AXES, None, None),
            P(rows, None, None),
            P(rows, None),
            P(rows, None, None),
            P(rows, None, None),
            P(rows),
        ),
        out_specs=(P(rows, None), P(rows, None, None)),
        check_vma=False,
    )
```

```python
import functools

import jax
import jax.numpy as jnp
from jax import lax
from jax.experimental import pallas as pl
from jax.experimental.pallas import tpu as pltpu
from jax.sharding import PartitionSpec as P

score_scale = 192.0 ** (-0.5)
EXPERT_AXES = ("node", "local", "pair")
LANES = 128
VMEM_LIMIT = 8 * 2**20


def slot_tables(picked, weights, experts, capacity):
    row_count, choose = picked.shape
    flat_picks = picked.reshape(-1)
    matches = (flat_picks[:, None] == jnp.arange(experts, dtype=jnp.int32)[None, :]).astype(
        jnp.int32
    )
    earlier = jnp.cumsum(matches, axis=0) - matches
    position = jnp.sum(earlier * matches, axis=1)
    slot_index = flat_picks * capacity + position
    slot_hits = (
        slot_index[:, None] == jnp.arange(experts * capacity, dtype=jnp.int32)[None, :]
    ).astype(jnp.float32)
    owner = (
        jnp.arange(row_count * choose, dtype=jnp.int32)[:, None] // choose
        == jnp.arange(row_count, dtype=jnp.int32)[None, :]
    ).astype(jnp.float32)
    dispatch = jnp.dot(slot_hits.T, owner, precision=lax.Precision.HIGHEST)
    combine = jnp.dot(
        owner.T,
        slot_hits * weights.astype(jnp.float32).reshape(-1)[:, None],
        precision=lax.Precision.HIGHEST,
    )
    return (dispatch, combine)


def attend_core(first, limits, ql_ref, qr_ref, cl_ref, cr_ref, out_ref, pairs_ref, rotary_ref):
    rows, heads, _ = ql_ref.shape
    rope, context = cr_ref.shape[1:]
    all_rows, width = qr_ref.shape
    place = lax.broadcasted_iota(jnp.int32, (heads, context), 1)
    pairs = width // (2 * rope)
    for p in range(pairs):
        pairs_ref[pl.ds(p * all_rows, all_rows), :] = qr_ref[
            :, p * 2 * rope : (p + 1) * 2 * rope
        ].astype(jnp.float32)
    for r in range(rows):
        both = pairs_ref[pl.ds(first + r, pairs, stride=all_rows), :].astype(jnp.bfloat16)
        for odd in range(2):
            rotary_ref[r, pl.ds(odd, pairs, stride=2), :] = jnp.dot(
                both[:, odd * rope : (odd + 1) * rope],
                cr_ref[r],
                preferred_element_type=jnp.float32,
            )
    scores = []
    for r in range(rows):
        s = lax.dot_general(
            ql_ref[r], cl_ref[r], (((1,), (1,)), ((), ())), preferred_element_type=jnp.float32
        )
        s = (s + rotary_ref[r]) * score_scale
        scores.append(jnp.where(place < limits[r], s, -1e30))
    probs = []
    for s in scores:
        exponent = jnp.exp(s - jnp.max(s, axis=1, keepdims=True))
        probs.append((exponent / jnp.sum(exponent, axis=1, keepdims=True)).astype(jnp.bfloat16))
    for r, p in enumerate(probs):
        out_ref[r] = jnp.dot(p, cl_ref[r], preferred_element_type=jnp.float32).astype(
            out_ref.dtype
        )


def fetch(sources, targets, sems):
    copies = [
        pltpu.make_async_copy(source, target, sems.at[i])
        for i, (source, target) in enumerate(zip(sources, targets))
    ]
    for copy in copies:
        copy.start()
    return copies


def attend_kernel(split, lengths_hbm, ql_hbm, qr_hbm, cl_hbm, cr_hbm, out_hbm, *refs):
    limits_ref, ql_late, qr_ref, cl_late, cr_late = refs[:5]
    lengths_ref, ql_ref, cl_ref, cr_ref, out_ref, pairs_ref, rotary_ref, sems, late_sems = refs[5:]
    part, late = pl.ds(0, split), pl.ds(split, ql_late.shape[0])
    copies = fetch(
        (lengths_hbm, qr_hbm, cr_hbm.at[part], cl_hbm.at[part], ql_hbm.at[part]),
        (lengths_ref, qr_ref, cr_ref, cl_ref, ql_ref),
        sems,
    )
    late_copies = fetch(
        (cr_hbm.at[late], cl_hbm.at[late], ql_hbm.at[late]), (cr_late, cl_late, ql_late), late_sems
    )
    for copy in copies:
        copy.wait()
    for r in range(limits_ref.shape[0]):
        limits_ref[pl.ds(r, 1), :] = jnp.full(
            (1, limits_ref.shape[1]), lengths_ref[split + r], jnp.int32
        )
    limits = [lengths_ref[r] for r in range(split)]
    attend_core(0, limits, ql_ref, qr_ref, cl_ref, cr_ref, out_ref, pairs_ref, rotary_ref)
    for copy in fetch((out_ref,), (out_hbm.at[part],), sems) + late_copies:
        copy.wait()


def staged_kernel(first, limits_ref, ql_ref, qr_ref, cl_ref, cr_ref, so_far, out_hbm, *scratch):
    out_ref, pairs_ref, rotary_ref, sems = scratch
    rows = ql_ref.shape[0]
    limits = [limits_ref[pl.ds(r, 1), :] for r in range(rows)]
    attend_core(first, limits, ql_ref, qr_ref, cl_ref, cr_ref, out_ref, pairs_ref, rotary_ref)
    for copy in fetch((out_ref,), (out_hbm.at[pl.ds(first, rows)],), sems):
        copy.wait()


def attend_cost(count, heads, context, latent, rope):
    return pl.CostEstimate(
        flops=2 * count * heads * context * (2 * latent + rope),
        bytes_accessed=10 * count * latent * (2 * heads + context),
        transcendentals=count * heads * context,
    )


ANYWHERE = pl.BlockSpec(memory_space=pl.ANY)
IN_VMEM = pl.BlockSpec(memory_space=pltpu.VMEM)


def attend_first(split, query_latent, query_rope, cache_latent, cache_rope, lengths):
    row_count, heads, latent = query_latent.shape
    rope, context = cache_rope.shape[1:]
    operands = (lengths, query_latent, query_rope, cache_latent, cache_rope)
    late = row_count - split

    def held(count):
        return [
            pltpu.VMEM((count, heads, latent), jnp.bfloat16),
            pltpu.VMEM((count, context, latent), jnp.bfloat16),
            pltpu.VMEM((count, rope, context), jnp.bfloat16),
        ]

    ql_late, cl_late, cr_late = held(late)
    out = pl.pallas_call(
        functools.partial(attend_kernel, split),
        out_shape=[
            pltpu.HBM((row_count, heads, latent), jnp.bfloat16),
            pltpu.VMEM((late, context), jnp.int32),
            ql_late,
            pltpu.VMEM(query_rope.shape, jnp.bfloat16),
            cl_late,
            cr_late,
        ],
        in_specs=[ANYWHERE] * 5,
        out_specs=[ANYWHERE] + [IN_VMEM] * 5,
        scratch_shapes=[pltpu.SMEM(lengths.shape, lengths.dtype)]
        + held(split)
        + [
            pltpu.VMEM((split, heads, latent), jnp.bfloat16),
            pltpu.VMEM((row_count * heads // 2, 2 * rope), jnp.float32),
            pltpu.VMEM((split, heads, context), jnp.float32),
            pltpu.SemaphoreType.DMA((5,)),
            pltpu.SemaphoreType.DMA((3,)),
        ],
        compiler_params=pltpu.CompilerParams(vmem_limit_bytes=(row_count + 4) * 2**20),
        cost_estimate=attend_cost(split, heads, context, latent, rope),
    )(*map(in_hbm, operands))
    return out[0], out[1:]


def attend_staged(first, staged, so_far):
    limits, query_latent, query_rope, cache_latent, cache_rope = staged
    count, heads, latent = query_latent.shape
    rope, context = cache_rope.shape[1:]
    return pl.pallas_call(
        functools.partial(staged_kernel, first),
        out_shape=pltpu.HBM(so_far.shape, so_far.dtype),
        in_specs=[IN_VMEM] * 5 + [ANYWHERE],
        out_specs=ANYWHERE,
        scratch_shapes=[
            pltpu.VMEM((count, heads, latent), jnp.bfloat16),
            pltpu.VMEM((so_far.shape[0] * heads // 2, 2 * rope), jnp.float32),
            pltpu.VMEM((count, heads, context), jnp.float32),
            pltpu.SemaphoreType.DMA((1,)),
        ],
        input_output_aliases={5: 0},
        compiler_params=pltpu.CompilerParams(vmem_limit_bytes=(count + 4) * 2**20),
        cost_estimate=attend_cost(count, heads, context, latent, rope),
    )(*map(in_vmem, staged), so_far)


def load_kernel(source_hbm, target_ref, sems):
    step = source_hbm.shape[0] // sems.shape[0]
    cuts = [pl.ds(i * step, step) for i in range(sems.shape[0])]
    for copy in fetch(
        [source_hbm.at[cut] for cut in cuts], [target_ref.at[cut] for cut in cuts], sems
    ):
        copy.wait()


def load(matrix):
    return pl.pallas_call(
        load_kernel,
        out_shape=pltpu.VMEM(matrix.shape, matrix.dtype),
        in_specs=[ANYWHERE],
        out_specs=IN_VMEM,
        scratch_shapes=[pltpu.SemaphoreType.DMA((4 if matrix.shape[0] % 64 == 0 else 1,))],
        compiler_params=pltpu.CompilerParams(vmem_limit_bytes=2**20),
        cost_estimate=pl.CostEstimate(
            flops=0, bytes_accessed=2 * matrix.size, transcendentals=0
        ),
    )(in_hbm(matrix))


def in_hbm(value):
    return pltpu.with_memory_space_constraint(value, pltpu.HBM)


def in_vmem(value):
    return pltpu.with_memory_space_constraint(value, pltpu.VMEM)


def expert_by_slots(tokens, expert_ids, combine_weights, expert_weight):
    row_count, model_width = tokens.shape
    choose = expert_ids.shape[1]
    experts = lax.axis_size(EXPERT_AXES)
    capacity = min(row_count, 3 * max(1, (row_count * choose + experts - 1) // experts))
    matrix = expert_weight[0]
    dispatch, combine = slot_tables(expert_ids, combine_weights, experts, capacity)
    outgoing = jnp.dot(
        dispatch.astype(jnp.bfloat16), tokens, preferred_element_type=jnp.float32
    ).astype(jnp.bfloat16)
    outgoing = outgoing.reshape(experts, capacity, model_width)
    received = lax.all_to_all(outgoing, EXPERT_AXES, split_axis=0, concat_axis=0, tiled=True)
    hidden = jnp.dot(received.reshape(-1, model_width), matrix, preferred_element_type=jnp.float32)
    returned = lax.all_to_all(
        jax.nn.silu(hidden).astype(jnp.bfloat16).reshape(received.shape[:-1] + (matrix.shape[1],)),
        EXPERT_AXES,
        split_axis=0,
        concat_axis=0,
        tiled=True,
    )
    returned = returned.reshape(experts * capacity, -1).astype(jnp.float32)
    mixture = jnp.dot(combine, returned, precision=lax.Precision.HIGHEST)
    return mixture.astype(jnp.bfloat16)


def payload_kernel(
    ids_hbm, weights_hbm, tokens_hbm, out_ref, ids_ref, weights_ref, sems
):
    choose, rows = ids_ref.shape
    width = tokens_hbm.shape[1]
    copies = [
        pltpu.make_async_copy(ids_hbm, ids_ref, sems.at[0]),
        pltpu.make_async_copy(weights_hbm, weights_ref, sems.at[1]),
        pltpu.make_async_copy(tokens_hbm, out_ref.at[:, pl.ds(0, width)], sems.at[2]),
    ]
    for copy in copies:
        copy.start()
    copies[0].wait()
    copies[1].wait()
    expert = lax.broadcasted_iota(jnp.int32, (LANES, rows), 0)
    table = jnp.zeros((LANES, rows), jnp.float32)
    ids, weights = ids_ref[...], weights_ref[...].astype(jnp.float32)
    for k in range(choose):
        table = table + jnp.where(expert == ids[k : k + 1], weights[k : k + 1], 0.0)
    eye = (
        lax.broadcasted_iota(jnp.int32, (rows, rows), 0)
        == lax.broadcasted_iota(jnp.int32, (rows, rows), 1)
    ).astype(jnp.bfloat16)
    out_ref[:, width:] = lax.dot_general(
        eye,
        table.astype(jnp.bfloat16),
        (((1,), (1,)), ((), ())),
        preferred_element_type=jnp.float32,
    ).astype(jnp.bfloat16)
    copies[2].wait()


def make_payload(tokens, expert_ids, combine_weights):
    rows, width = tokens.shape
    choose = expert_ids.shape[1]
    return pl.pallas_call(
        payload_kernel,
        out_shape=pltpu.VMEM((rows, width + LANES), jnp.bfloat16),
        in_specs=[pl.BlockSpec(memory_space=pl.ANY)] * 3,
        out_specs=pl.BlockSpec(memory_space=pltpu.VMEM),
        scratch_shapes=[
            pltpu.VMEM((choose, rows), jnp.int32),
            pltpu.VMEM((choose, rows), jnp.bfloat16),
            pltpu.SemaphoreType.DMA((3,)),
        ],
        compiler_params=pltpu.CompilerParams(vmem_limit_bytes=4 * 2**20),
        cost_estimate=pl.CostEstimate(
            flops=0, bytes_accessed=4 * rows * width, transcendentals=0
        ),
    )(in_hbm(expert_ids.T), in_hbm(combine_weights.T), in_hbm(tokens))


def expert_kernel(count, *refs):
    here = lax.axis_index(EXPERT_AXES).astype(jnp.int32)
    blocks, matrices = refs[:count], refs[count : count + 2]
    near_ref, far_ref = refs[count + 2 :]
    width, hidden = matrices[0].shape
    rows = jnp.concatenate([block[...] for block in blocks], axis=0)
    features, shares = rows[:, :width], rows[:, width:].astype(jnp.float32)
    lane = lax.broadcasted_iota(jnp.int32, shares.shape, 1)
    share = [
        jnp.sum(jnp.where(lane == (here ^ which), shares, 0.0), axis=1, keepdims=True)
        for which in range(2)
    ]
    half = near_ref.shape[0]
    tile = 256
    for n in range(0, hidden, tile):
        total = None
        for which, matrix_ref in enumerate(matrices):
            value = jnp.dot(
                features, matrix_ref[:, n : n + tile], preferred_element_type=jnp.float32
            )
            term = share[which] * (value / (1.0 + jnp.exp(-value)))
            total = term if total is None else total + term
        near_ref[:, n : n + tile] = total[:half]
        far_ref[:, n : n + tile] = total[half:].astype(jnp.bfloat16)


def serve(blocks, own, other):
    count = len(blocks)
    rows = blocks[0].shape[0]
    width, hidden = own.shape
    whole = pl.BlockSpec(memory_space=pltpu.VMEM)
    half = count // 2 * rows
    return pl.pallas_call(
        functools.partial(expert_kernel, count),
        out_shape=[
            pltpu.VMEM((half, hidden), jnp.float32),
            pltpu.VMEM((half, hidden), jnp.bfloat16),
        ],
        in_specs=[whole] * (count + 2),
        out_specs=[whole] * 2,
        compiler_params=pltpu.CompilerParams(vmem_limit_bytes=VMEM_LIMIT),
        cost_estimate=pl.CostEstimate(
            flops=4 * count * rows * width * hidden,
            bytes_accessed=4 * width * hidden,
            transcendentals=2 * count * rows * hidden,
        ),
    )(*map(in_vmem, blocks), in_vmem(own), in_vmem(other))


def swap(value, axis, size, mask):
    return lax.ppermute(value, axis, [(i, i ^ mask) for i in range(size)])


def tie(value, *others):
    return lax.optimization_barrier((value,) + others)[0]


def gathered(attention, tokens, expert_ids, combine_weights, expert_weight):
    nodes, locals_, pairs = (lax.axis_size(axis) for axis in EXPERT_AXES)
    rows = tokens.shape[0]
    own = expert_weight[0]
    other = swap(own, "pair", pairs, 1)

    query_latent, query_rope, cache_latent, cache_rope, lengths = attention
    mine = make_payload(tokens, expert_ids, combine_weights)
    near, far = {0: mine}, {}
    near[1] = swap(mine, "node", nodes, 1)
    far[0] = swap(mine, "local", locals_, 1)
    near[2] = swap(mine, "node", nodes, 2)
    count = query_latent.shape[0]
    half = count // 2
    rest = (query_rope, cache_latent, cache_rope, lengths)
    attended, staged = attend_first(half, tie(query_latent, mine), *rest)
    near[1], far[0], near[2], _ = lax.optimization_barrier((near[1], far[0], near[2], attended))
    near[3] = swap(near[2], "node", nodes, 1)
    far[2] = swap(near[2], "local", locals_, 1)
    far[1] = swap(far[0], "node", nodes, 1)
    far[3] = swap(near[3], "local", locals_, 1)
    own = load(tie(own, near[3]))
    far[1], far[2], far[3], _ = lax.optimization_barrier((far[1], far[2], far[3], own))
    blocks = [near[n] for n in range(nodes)] + [far[n] for n in range(nodes)]
    kept, sent = serve(blocks, own, other)
    came = swap(sent, "local", locals_, 1)
    attended = attend_staged(half, staged, tie(attended, sent))
    came = tie(came, attended)
    kept = kept.reshape(nodes, rows, -1)
    came = came.reshape(nodes, rows, -1)
    total = kept[0] + came[0].astype(jnp.float32)
    for n in (2, 1, 3):
        part = (kept[n] + came[n].astype(jnp.float32)).astype(jnp.bfloat16)
        total = total + swap(part, "node", nodes, n).astype(jnp.float32)
    return total.astype(jnp.bfloat16), attended


def body(
    tokens,
    expert_ids,
    combine_weights,
    expert_weight,
    query_latent,
    query_rope,
    cache_latent,
    cache_rope,
    lengths,
):
    sizes = tuple(lax.axis_size(axis) for axis in EXPERT_AXES)
    attention = (query_latent, query_rope, cache_latent, cache_rope, lengths)
    if sizes == (4, 2, 2):
        return gathered(attention, tokens, expert_ids, combine_weights, expert_weight)
    half = query_latent.shape[0] // 2
    attended, staged = attend_first(half, *attention)
    attended = attend_staged(half, staged, attended)
    expert_mix = expert_by_slots(tokens, expert_ids, combine_weights, expert_weight)
    return (expert_mix, attended)


def solution(mesh):
    rows = ("group",) + EXPERT_AXES
    return jax.shard_map(
        body,
        mesh=mesh,
        in_specs=(
            P(rows, None),
            P(rows, None),
            P(rows, None),
            P(EXPERT_AXES, None, None),
            P(rows, None, None),
            P(rows, None),
            P(rows, None, None),
            P(rows, None, None),
            P(rows),
        ),
        out_specs=(P(rows, None), P(rows, None, None)),
        check_vma=False,
    )
```

```python
import functools

import jax
import jax.numpy as jnp
from jax import lax
from jax.experimental import pallas as pl
from jax.experimental.pallas import tpu as pltpu
from jax.sharding import PartitionSpec as P

score_scale = 192.0 ** (-0.5)
EXPERT_AXES = ("node", "local", "pair")
LANES = 128
VMEM_LIMIT = 8 * 2**20


def slot_tables(picked, weights, experts, capacity):
    row_count, choose = picked.shape
    flat_picks = picked.reshape(-1)
    matches = (flat_picks[:, None] == jnp.arange(experts, dtype=jnp.int32)[None, :]).astype(
        jnp.int32
    )
    earlier = jnp.cumsum(matches, axis=0) - matches
    position = jnp.sum(earlier * matches, axis=1)
    slot_index = flat_picks * capacity + position
    slot_hits = (
        slot_index[:, None] == jnp.arange(experts * capacity, dtype=jnp.int32)[None, :]
    ).astype(jnp.float32)
    owner = (
        jnp.arange(row_count * choose, dtype=jnp.int32)[:, None] // choose
        == jnp.arange(row_count, dtype=jnp.int32)[None, :]
    ).astype(jnp.float32)
    dispatch = jnp.dot(slot_hits.T, owner, precision=lax.Precision.HIGHEST)
    combine = jnp.dot(
        owner.T,
        slot_hits * weights.astype(jnp.float32).reshape(-1)[:, None],
        precision=lax.Precision.HIGHEST,
    )
    return (dispatch, combine)


def attend_core(first, limits, ql_ref, qr_ref, cl_ref, cr_ref, out_ref, pairs_ref, rotary_ref):
    rows, heads, _ = ql_ref.shape
    rope, context = cr_ref.shape[1:]
    all_rows, width = qr_ref.shape
    place = lax.broadcasted_iota(jnp.int32, (heads, context), 1)
    pairs = width // (2 * rope)
    for p in range(pairs):
        pairs_ref[pl.ds(p * all_rows, all_rows), :] = qr_ref[
            :, p * 2 * rope : (p + 1) * 2 * rope
        ].astype(jnp.float32)
    for r in range(rows):
        both = pairs_ref[pl.ds(first + r, pairs, stride=all_rows), :].astype(jnp.bfloat16)
        for odd in range(2):
            rotary_ref[r, pl.ds(odd, pairs, stride=2), :] = jnp.dot(
                both[:, odd * rope : (odd + 1) * rope],
                cr_ref[r],
                preferred_element_type=jnp.float32,
            )
    scores = []
    for r in range(rows):
        s = lax.dot_general(
            ql_ref[r], cl_ref[r], (((1,), (1,)), ((), ())), preferred_element_type=jnp.float32
        )
        s = (s + rotary_ref[r]) * score_scale
        scores.append(jnp.where(place < limits[r], s, -1e30))
    probs = []
    for s in scores:
        exponent = jnp.exp(s - jnp.max(s, axis=1, keepdims=True))
        probs.append((exponent / jnp.sum(exponent, axis=1, keepdims=True)).astype(jnp.bfloat16))
    for r, p in enumerate(probs):
        out_ref[r] = jnp.dot(p, cl_ref[r], preferred_element_type=jnp.float32).astype(
            out_ref.dtype
        )


def fetch(sources, targets, sems):
    copies = [
        pltpu.make_async_copy(source, target, sems.at[i])
        for i, (source, target) in enumerate(zip(sources, targets))
    ]
    for copy in copies:
        copy.start()
    return copies


def attend_kernel(split, lengths_hbm, ql_hbm, qr_hbm, cl_hbm, cr_hbm, out_hbm, *refs):
    limits_ref, ql_late, qr_ref, cl_late, cr_late = refs[:5]
    lengths_ref, ql_ref, cl_ref, cr_ref, out_ref, pairs_ref, rotary_ref, sems, late_sems = refs[5:]
    part, late = pl.ds(0, split), pl.ds(split, ql_late.shape[0])
    copies = fetch(
        (lengths_hbm, qr_hbm, cr_hbm.at[part], cl_hbm.at[part], ql_hbm.at[part]),
        (lengths_ref, qr_ref, cr_ref, cl_ref, ql_ref),
        sems,
    )
    late_copies = fetch(
        (cr_hbm.at[late], cl_hbm.at[late], ql_hbm.at[late]), (cr_late, cl_late, ql_late), late_sems
    )
    for copy in copies:
        copy.wait()
    for r in range(limits_ref.shape[0]):
        limits_ref[pl.ds(r, 1), :] = jnp.full(
            (1, limits_ref.shape[1]), lengths_ref[split + r], jnp.int32
        )
    limits = [lengths_ref[r] for r in range(split)]
    attend_core(0, limits, ql_ref, qr_ref, cl_ref, cr_ref, out_ref, pairs_ref, rotary_ref)
    for copy in fetch((out_ref,), (out_hbm.at[part],), sems) + late_copies:
        copy.wait()


def staged_kernel(first, limits_ref, ql_ref, qr_ref, cl_ref, cr_ref, so_far, out_hbm, *scratch):
    out_ref, pairs_ref, rotary_ref, sems = scratch
    rows = ql_ref.shape[0]
    limits = [limits_ref[pl.ds(r, 1), :] for r in range(rows)]
    attend_core(first, limits, ql_ref, qr_ref, cl_ref, cr_ref, out_ref, pairs_ref, rotary_ref)
    for copy in fetch((out_ref,), (out_hbm.at[pl.ds(first, rows)],), sems):
        copy.wait()


def attend_cost(count, heads, context, latent, rope):
    return pl.CostEstimate(
        flops=2 * count * heads * context * (2 * latent + rope),
        bytes_accessed=10 * count * latent * (2 * heads + context),
        transcendentals=count * heads * context,
    )


ANYWHERE = pl.BlockSpec(memory_space=pl.ANY)
IN_VMEM = pl.BlockSpec(memory_space=pltpu.VMEM)


def attend_first(split, query_latent, query_rope, cache_latent, cache_rope, lengths):
    row_count, heads, latent = query_latent.shape
    rope, context = cache_rope.shape[1:]
    operands = (lengths, query_latent, query_rope, cache_latent, cache_rope)
    late = row_count - split

    def held(count):
        return [
            pltpu.VMEM((count, heads, latent), jnp.bfloat16),
            pltpu.VMEM((count, context, latent), jnp.bfloat16),
            pltpu.VMEM((count, rope, context), jnp.bfloat16),
        ]

    ql_late, cl_late, cr_late = held(late)
    out = pl.pallas_call(
        functools.partial(attend_kernel, split),
        out_shape=[
            pltpu.HBM((row_count, heads, latent), jnp.bfloat16),
            pltpu.VMEM((late, context), jnp.int32),
            ql_late,
            pltpu.VMEM(query_rope.shape, jnp.bfloat16),
            cl_late,
            cr_late,
        ],
        in_specs=[ANYWHERE] * 5,
        out_specs=[ANYWHERE] + [IN_VMEM] * 5,
        scratch_shapes=[pltpu.SMEM(lengths.shape, lengths.dtype)]
        + held(split)
        + [
            pltpu.VMEM((split, heads, latent), jnp.bfloat16),
            pltpu.VMEM((row_count * heads // 2, 2 * rope), jnp.float32),
            pltpu.VMEM((split, heads, context), jnp.float32),
            pltpu.SemaphoreType.DMA((5,)),
            pltpu.SemaphoreType.DMA((3,)),
        ],
        compiler_params=pltpu.CompilerParams(vmem_limit_bytes=(row_count + 4) * 2**20),
        cost_estimate=attend_cost(split, heads, context, latent, rope),
    )(*map(in_hbm, operands))
    return out[0], out[1:]


def attend_staged(first, staged, so_far):
    limits, query_latent, query_rope, cache_latent, cache_rope = staged
    count, heads, latent = query_latent.shape
    rope, context = cache_rope.shape[1:]
    return pl.pallas_call(
        functools.partial(staged_kernel, first),
        out_shape=pltpu.HBM(so_far.shape, so_far.dtype),
        in_specs=[IN_VMEM] * 5 + [ANYWHERE],
        out_specs=ANYWHERE,
        scratch_shapes=[
            pltpu.VMEM((count, heads, latent), jnp.bfloat16),
            pltpu.VMEM((so_far.shape[0] * heads // 2, 2 * rope), jnp.float32),
            pltpu.VMEM((count, heads, context), jnp.float32),
            pltpu.SemaphoreType.DMA((1,)),
        ],
        input_output_aliases={5: 0},
        compiler_params=pltpu.CompilerParams(vmem_limit_bytes=(count + 4) * 2**20),
        cost_estimate=attend_cost(count, heads, context, latent, rope),
    )(*map(in_vmem, staged), so_far)


def load_kernel(source_hbm, target_ref, sems):
    step = source_hbm.shape[0] // sems.shape[0]
    cuts = [pl.ds(i * step, step) for i in range(sems.shape[0])]
    for copy in fetch(
        [source_hbm.at[cut] for cut in cuts], [target_ref.at[cut] for cut in cuts], sems
    ):
        copy.wait()


def load(matrix):
    return pl.pallas_call(
        load_kernel,
        out_shape=pltpu.VMEM(matrix.shape, matrix.dtype),
        in_specs=[ANYWHERE],
        out_specs=IN_VMEM,
        scratch_shapes=[pltpu.SemaphoreType.DMA((4 if matrix.shape[0] % 64 == 0 else 1,))],
        compiler_params=pltpu.CompilerParams(vmem_limit_bytes=2**20),
        cost_estimate=pl.CostEstimate(
            flops=0, bytes_accessed=2 * matrix.size, transcendentals=0
        ),
    )(in_hbm(matrix))


def in_hbm(value):
    return pltpu.with_memory_space_constraint(value, pltpu.HBM)


def in_vmem(value):
    return pltpu.with_memory_space_constraint(value, pltpu.VMEM)


def expert_by_slots(tokens, expert_ids, combine_weights, expert_weight):
    row_count, model_width = tokens.shape
    choose = expert_ids.shape[1]
    experts = lax.axis_size(EXPERT_AXES)
    capacity = min(row_count, 3 * max(1, (row_count * choose + experts - 1) // experts))
    matrix = expert_weight[0]
    dispatch, combine = slot_tables(expert_ids, combine_weights, experts, capacity)
    outgoing = jnp.dot(
        dispatch.astype(jnp.bfloat16), tokens, preferred_element_type=jnp.float32
    ).astype(jnp.bfloat16)
    outgoing = outgoing.reshape(experts, capacity, model_width)
    received = lax.all_to_all(outgoing, EXPERT_AXES, split_axis=0, concat_axis=0, tiled=True)
    hidden = jnp.dot(received.reshape(-1, model_width), matrix, preferred_element_type=jnp.float32)
    returned = lax.all_to_all(
        jax.nn.silu(hidden).astype(jnp.bfloat16).reshape(received.shape[:-1] + (matrix.shape[1],)),
        EXPERT_AXES,
        split_axis=0,
        concat_axis=0,
        tiled=True,
    )
    returned = returned.reshape(experts * capacity, -1).astype(jnp.float32)
    mixture = jnp.dot(combine, returned, precision=lax.Precision.HIGHEST)
    return mixture.astype(jnp.bfloat16)


def payload_kernel(
    ids_hbm, weights_hbm, tokens_hbm, out_ref, ids_ref, weights_ref, sems
):
    choose, rows = ids_ref.shape
    width = tokens_hbm.shape[1]
    copies = [
        pltpu.make_async_copy(ids_hbm, ids_ref, sems.at[0]),
        pltpu.make_async_copy(weights_hbm, weights_ref, sems.at[1]),
        pltpu.make_async_copy(tokens_hbm, out_ref.at[:, pl.ds(0, width)], sems.at[2]),
    ]
    for copy in copies:
        copy.start()
    copies[0].wait()
    copies[1].wait()
    expert = lax.broadcasted_iota(jnp.int32, (LANES, rows), 0)
    table = jnp.zeros((LANES, rows), jnp.float32)
    ids, weights = ids_ref[...], weights_ref[...].astype(jnp.float32)
    for k in range(choose):
        table = table + jnp.where(expert == ids[k : k + 1], weights[k : k + 1], 0.0)
    eye = (
        lax.broadcasted_iota(jnp.int32, (rows, rows), 0)
        == lax.broadcasted_iota(jnp.int32, (rows, rows), 1)
    ).astype(jnp.bfloat16)
    out_ref[:, width:] = lax.dot_general(
        eye,
        table.astype(jnp.bfloat16),
        (((1,), (1,)), ((), ())),
        preferred_element_type=jnp.float32,
    ).astype(jnp.bfloat16)
    copies[2].wait()


def make_payload(tokens, expert_ids, combine_weights):
    rows, width = tokens.shape
    choose = expert_ids.shape[1]
    return pl.pallas_call(
        payload_kernel,
        out_shape=pltpu.VMEM((rows, width + LANES), jnp.bfloat16),
        in_specs=[pl.BlockSpec(memory_space=pl.ANY)] * 3,
        out_specs=pl.BlockSpec(memory_space=pltpu.VMEM),
        scratch_shapes=[
            pltpu.VMEM((choose, rows), jnp.int32),
            pltpu.VMEM((choose, rows), jnp.bfloat16),
            pltpu.SemaphoreType.DMA((3,)),
        ],
        compiler_params=pltpu.CompilerParams(vmem_limit_bytes=4 * 2**20),
        cost_estimate=pl.CostEstimate(
            flops=0, bytes_accessed=4 * rows * width, transcendentals=0
        ),
    )(in_hbm(expert_ids.T), in_hbm(combine_weights.T), in_hbm(tokens))


def expert_kernel(count, *refs):
    here = lax.axis_index(EXPERT_AXES).astype(jnp.int32)
    blocks, matrices = refs[:count], refs[count : count + 2]
    kept_ref, *sent_refs = refs[count + 2 :]
    width, hidden = matrices[0].shape
    rows = jnp.concatenate([block[...] for block in blocks], axis=0)
    features, shares = rows[:, :width], rows[:, width:].astype(jnp.float32)
    lane = lax.broadcasted_iota(jnp.int32, shares.shape, 1)
    share = [
        jnp.sum(jnp.where(lane == (here ^ which), shares, 0.0), axis=1, keepdims=True)
        for which in range(2)
    ]
    step = kept_ref.shape[0]
    tile = 256
    for n in range(0, hidden, tile):
        total = None
        for which, matrix_ref in enumerate(matrices):
            value = jnp.dot(
                features, matrix_ref[:, n : n + tile], preferred_element_type=jnp.float32
            )
            term = share[which] * (value / (1.0 + jnp.exp(-value)))
            total = term if total is None else total + term
        kept_ref[:, n : n + tile] = total[:step]
        for i, sent_ref in enumerate(sent_refs, 1):
            sent_ref[:, n : n + tile] = total[i * step : (i + 1) * step].astype(jnp.bfloat16)


def serve(blocks, own, other):
    count = len(blocks)
    rows = blocks[0].shape[0]
    width, hidden = own.shape
    whole = pl.BlockSpec(memory_space=pltpu.VMEM)
    pair = 2 * rows
    return pl.pallas_call(
        functools.partial(expert_kernel, count),
        out_shape=[
            pltpu.VMEM((pair, hidden), jnp.float32),
        ]
        + [pltpu.VMEM((pair, hidden), jnp.bfloat16)] * (count // 2 - 1),
        in_specs=[whole] * (count + 2),
        out_specs=[whole] * (count // 2),
        compiler_params=pltpu.CompilerParams(vmem_limit_bytes=VMEM_LIMIT),
        cost_estimate=pl.CostEstimate(
            flops=4 * count * rows * width * hidden,
            bytes_accessed=4 * width * hidden,
            transcendentals=2 * count * rows * hidden,
        ),
    )(*map(in_vmem, blocks), in_vmem(own), in_vmem(other))


def swap(value, axis, size, mask):
    return lax.ppermute(value, axis, [(i, i ^ mask) for i in range(size)])


def tie(value, *others):
    return lax.optimization_barrier((value,) + others)[0]


def gathered(attention, tokens, expert_ids, combine_weights, expert_weight):
    nodes, locals_, pairs = (lax.axis_size(axis) for axis in EXPERT_AXES)
    rows = tokens.shape[0]
    own = expert_weight[0]
    other = swap(own, "pair", pairs, 1)

    query_latent, query_rope, cache_latent, cache_rope, lengths = attention
    mine = make_payload(tokens, expert_ids, combine_weights)
    near, far = {0: mine}, {}
    near[1] = swap(mine, "node", nodes, 1)
    far[0] = swap(mine, "local", locals_, 1)
    near[2] = swap(mine, "node", nodes, 2)
    count = query_latent.shape[0]
    half = count // 2
    rest = (query_rope, cache_latent, cache_rope, lengths)
    attended, staged = attend_first(half, tie(query_latent, mine), *rest)
    near[1], far[0], near[2], _ = lax.optimization_barrier((near[1], far[0], near[2], attended))
    near[3] = swap(near[2], "node", nodes, 1)
    far[2] = swap(near[2], "local", locals_, 1)
    far[1] = swap(far[0], "node", nodes, 1)
    far[3] = swap(near[3], "local", locals_, 1)
    own = load(tie(own, near[3]))
    far[1], far[2], far[3], _ = lax.optimization_barrier((far[1], far[2], far[3], own))
    blocks = [block for n in range(nodes) for block in (near[n], far[n])]
    total, *sent = serve(blocks, own, other)
    came = [swap(sent[n - 1], "node", nodes, n) for n in (2, 3, 1)]
    attended = attend_staged(half, staged, tie(attended, *sent))
    came = lax.optimization_barrier(came + [attended])
    attended = came.pop()
    for value in came:
        total = total + value.astype(jnp.float32)
    came = swap(total[rows:].astype(jnp.bfloat16), "local", locals_, 1)
    total = total[:rows] + came.astype(jnp.float32)
    return total.astype(jnp.bfloat16), attended


def body(
    tokens,
    expert_ids,
    combine_weights,
    expert_weight,
    query_latent,
    query_rope,
    cache_latent,
    cache_rope,
    lengths,
):
    sizes = tuple(lax.axis_size(axis) for axis in EXPERT_AXES)
    attention = (query_latent, query_rope, cache_latent, cache_rope, lengths)
    if sizes == (4, 2, 2):
        return gathered(attention, tokens, expert_ids, combine_weights, expert_weight)
    half = query_latent.shape[0] // 2
    attended, staged = attend_first(half, *attention)
    attended = attend_staged(half, staged, attended)
    expert_mix = expert_by_slots(tokens, expert_ids, combine_weights, expert_weight)
    return (expert_mix, attended)


def solution(mesh):
    rows = ("group",) + EXPERT_AXES
    return jax.shard_map(
        body,
        mesh=mesh,
        in_specs=(
            P(rows, None),
            P(rows, None),
            P(rows, None),
            P(EXPERT_AXES, None, None),
            P(rows, None, None),
            P(rows, None),
            P(rows, None, None),
            P(rows, None, None),
            P(rows),
        ),
        out_specs=(P(rows, None), P(rows, None, None)),
        check_vma=False,
    )
```
